256 devices in a mesh: blk: 64 (over y, z, core), mp: 4 (over x).
Axes of the slice: x: 4, y: 4, z: 8, core: 2. Of those that a mesh axis runs over, the one named last changes fastest.
Arguments:
- hidden_states: bfloat16 [8192, 4096], P('blk', 'mp'), may hold values from -6 to 6
- expert_ids: int32 [8192, 1], P('blk'), may hold values from 0 to 31; in each aligned block of 128 rows (0 to 127, 128 to 255, ...) at most 5 rows name the same one
- probs: bfloat16 [8192, 1], P('blk'), may hold values from 0.049804688 to 0.59765625
- cotangent: bfloat16 [8192, 4096], P('blk', 'mp'), may hold values from -6 to 6
- w_gate: bfloat16 [49152, 4096], P(('blk', 'mp')), may hold values from -0.09375 to 0.09375
- w_up: bfloat16 [49152, 4096], P(('blk', 'mp')), may hold values from -0.09375 to 0.09375
- w_down: bfloat16 [49152, 4096], P(('blk', 'mp')), may hold values from -0.15625 to 0.15625
Outputs:
- mixed: bfloat16 [8192, 4096], P('blk', 'mp')
- grad_hidden: bfloat16 [8192, 4096], P('blk', 'mp')
- grad_probs: float32 [8192, 1], P('blk')
- grad_w_gate: bfloat16 [49152, 4096], P(('blk', 'mp'))
- grad_w_up: bfloat16 [49152, 4096], P(('blk', 'mp'))
- grad_w_down: bfloat16 [49152, 4096], P(('blk', 'mp'))
The draws below stay inside these ranges and needn't reach their ends.
Inputs may be any that keep to these rules, and one draw needn't show every extreme that they name: `expert_ids`: among the tokens of one index of blk (aligned blocks of 128 rows) no expert is named more than 5 times, and in every draw some expert is named exactly 5 times in some block.
All inputs are finite; a program needn't handle non-finite values.
Results may differ from the reference program's by a relative error of at most 0.017.
Values may be sent and summed in bfloat16 or wider, within the bound.
No kernel may reach another device: no remote copies, remote signals or barrier semaphores. Data moves between devices by JAX's collectives and lax.ppermute only.
A program may use at most 128 MiB of HBM per device.

```python
import math
import jax
import jax.numpy as jnp
import numpy as np
from jax import lax

D = 4096
FF = 1536
EXPERTS = 32
ROUTED = 1
TOK_DEV = 128
TOKENS = 8192
CAP = 5
SPAN = 192
N_BLK = 64


def level_of(rng, extent, split, least, top_value):
    level = 1.0
    for axis_at, parts in split:
        heights = jax.random.uniform(jax.random.fold_in(jax.random.fold_in(rng, 6), axis_at), (parts,), jnp.float32, least / len(split), top_value / len(split))
        level = level * jnp.repeat(jnp.exp(heights), extent[axis_at] // parts).reshape((-1,) + (1,) * (len(extent) - 1 - axis_at))
    return level


def shared_out(own_key, own, number, rows, number_of, top, reach, lean):
    order = jax.random.permutation(own_key, number_of)
    heavy_load, ordinary = shares(number_of, rows * top, reach, lean, True), shares(number_of, rows * top, reach, lean, False)
    places = jnp.arange(number_of)

    def named(sizes, turn):
        used = int((sizes > 0).sum())
        fixed = max(1, used // 4)
        moved = fixed + (places - fixed + turn * (used - fixed)) % max(1, number_of - fixed)
        return jnp.zeros((number_of,), jnp.int32).at[order[jnp.where(places < fixed, places, moved)]].set(jnp.asarray(sizes, jnp.int32))

    sizes = jnp.where(number % 4 == 0, named(heavy_load, number // 4), named(ordinary, number - number // 4 - 1))
    mixed = jax.random.permutation(jax.random.fold_in(own, 3), number_of)
    giver, taker = mixed[0:number_of // 2 * 2:2], mixed[1:number_of // 2 * 2:2]
    room = jnp.minimum(sizes[giver] - 1, reach - sizes[taker]) // 2
    room = jnp.where((giver == order[0]) | (taker == order[0]) | (sizes[taker] == 0), 0, jnp.maximum(room, 0))
    moved = jax.random.randint(jax.random.fold_in(own, 4), (number_of // 2,), 0, 1 << 20) % (room + 1)
    sizes = sizes.at[giver].add(-moved).at[taker].add(moved)
    members = jnp.searchsorted(jnp.cumsum(sizes), jnp.arange(rows * top), side="right").astype(jnp.int32)
    listing = members.reshape(top, rows).T
    listing = listing[jax.random.permutation(jax.random.fold_in(own, 1), rows)]
    turn = jax.random.randint(jax.random.fold_in(own, 2), (rows, 1), 0, top)
    return jnp.take_along_axis(listing, (jnp.arange(top)[None, :] + turn) % top, axis=1)


def shares(number_of, total, bound, slope, full):
    loads = [(1 << 20) // math.isqrt(grade ** slope) + 1 for grade in range(1, number_of + 1)]
    largest = bound if full else min(bound, max(-(-total // number_of), total * loads[0] // sum(loads)))
    least = 1 if total - largest >= number_of - 1 else 0
    counts, surplus = [largest] + [least] * (number_of - 1), total - largest - least * (number_of - 1)
    while surplus > 0:
        movable = [i for i in range(1, number_of) if counts[i] < largest] or [i for i in range(1, number_of) if counts[i] < bound]
        whole, remaining = sum([loads[i] for i in movable]), surplus
        for i in movable:
            extra = min(bound - counts[i], max(1, remaining * loads[i] // whole), surplus)
            counts[i] = counts[i] + extra
            surplus = surplus - extra
    return np.array(counts)


def scatter_about(key, extent, scale, reach, shards=(), kind=jnp.bfloat16):
    values = jax.random.normal(key, extent, jnp.float32) * scale
    if len(shards) > 0:
        values = level_of(key, extent, shards, -0.22, 0.18) * values
    return jnp.clip(values, min=-reach, max=reach).astype(kind)


def setup_inputs(seed: int = 0) -> dict:
    splits = jax.random.split(jax.random.key(seed), 8)
    hidden_states = scatter_about(splits[0], (TOKENS, D), 1.0, 6.0, ((0, 64), (1, 4)))
    expert_ids_keys = jax.random.split(jax.random.fold_in(splits[1], 1), TOKENS // TOK_DEV)
    expert_ids_turns = jax.random.permutation(jax.random.fold_in(splits[1], 3), TOKENS // TOK_DEV)
    expert_ids = jax.vmap(lambda own, number: shared_out(jax.random.fold_in(splits[1], 2), own, number, TOK_DEV, EXPERTS, ROUTED, CAP, 2))(expert_ids_keys, expert_ids_turns).reshape((TOKENS, ROUTED))
    probs = jnp.clip(jnp.exp(math.log(0.59765625) - 2.4849066 * jax.random.uniform(splits[2], (TOKENS, ROUTED), jnp.float32) ** level_of(splits[2], (TOKENS, ROUTED), ((0, 64),), -0.2, 0.2)), 0.049804688, 0.59765625).astype(jnp.bfloat16)
    cotangent = scatter_about(splits[3], (TOKENS, D), 1.0, 6.0, ((0, 64), (1, 4)))
    w_gate = scatter_about(splits[4], (EXPERTS * FF, D), D ** -0.5, 0.09375, ((0, 256),))
    w_up = scatter_about(splits[5], (EXPERTS * FF, D), D ** -0.5, 0.09375, ((0, 256),))
    w_down = scatter_about(splits[6], (EXPERTS * FF, D), FF ** -0.5, 0.15625, ((0, 256),))
    return {"hidden_states": hidden_states, "expert_ids": expert_ids, "probs": probs, "cotangent": cotangent, "w_gate": w_gate, "w_up": w_up, "w_down": w_down}


def block_terms(left_side, right_side):
    blocks = FF // SPAN
    rows_left = left_side.reshape(left_side.shape[0], blocks, SPAN).astype(jnp.float32)
    rows_right = right_side.reshape(blocks, SPAN, right_side.shape[1]).astype(jnp.float32)
    return jnp.einsum("gcf,cfd->cgd", rows_left, rows_right)


def rounded_sum(block_values):
    narrow = lax.optimization_barrier(block_values.astype(jnp.bfloat16))
    return jnp.sum(narrow.astype(jnp.float32), axis=0)


def reference(hidden_states, expert_ids, probs, cotangent, w_gate, w_up, w_down):
    pair_count = TOKENS * ROUTED
    group_rows = N_BLK * CAP
    flat_ids = expert_ids.reshape(pair_count).astype(jnp.int32)
    onehot = (flat_ids[:, None] == jnp.arange(EXPERTS, dtype=jnp.int32)[None, :]).astype(jnp.int32)
    running = jnp.cumsum(onehot.reshape(N_BLK, TOK_DEV * ROUTED, EXPERTS), axis=1).reshape(pair_count, EXPERTS)
    rank_in_group = jnp.sum((running - 1) * onehot, axis=1).astype(jnp.int32)
    shard_index = (jnp.arange(pair_count, dtype=jnp.int32) // (TOK_DEV * ROUTED)).astype(jnp.int32)
    slot_place = (shard_index * CAP + rank_in_group).astype(jnp.int32)
    slot_table = jnp.full((EXPERTS, group_rows), pair_count, jnp.int32)
    slot_table = slot_table.at[flat_ids, slot_place].set(jnp.arange(pair_count, dtype=jnp.int32))
    token_table = jnp.where(slot_table < pair_count, slot_table // ROUTED, TOKENS).astype(jnp.int32)
    zero_row = jnp.zeros((1, D), jnp.bfloat16)
    features = jnp.concatenate([hidden_states, zero_row], axis=0)
    grad_rows = jnp.concatenate([cotangent, zero_row], axis=0)
    pair_probs = jnp.concatenate([probs.reshape(pair_count), jnp.zeros((1,), jnp.bfloat16)], axis=0)

    def one_expert(expert):
        slot_x = features[token_table[expert]]
        slot_grad = grad_rows[token_table[expert]]
        slot_prob = pair_probs[slot_table[expert]]
        row_start = (expert * FF).astype(jnp.int32)
        gate_rows = lax.dynamic_slice_in_dim(w_gate, row_start, FF, 0)
        up_rows = lax.dynamic_slice_in_dim(w_up, row_start, FF, 0)
        down_rows = lax.dynamic_slice_in_dim(w_down, row_start, FF, 0)
        gate_pre = jnp.dot(slot_x, gate_rows.T, preferred_element_type=jnp.float32)
        up_pre = jnp.dot(slot_x, up_rows.T, preferred_element_type=jnp.float32)
        sigmoid_gate = jax.nn.sigmoid(gate_pre)
        activated = gate_pre * sigmoid_gate
        gated = (activated * up_pre).astype(jnp.bfloat16)
        expert_out = rounded_sum(block_terms(gated, down_rows))
        scaled = (slot_prob.astype(jnp.float32)[:, None] * slot_grad.astype(jnp.float32)).astype(jnp.bfloat16)
        grad_gated = jnp.dot(scaled, down_rows.T, preferred_element_type=jnp.float32)
        grad_gate_pre = (grad_gated * up_pre * sigmoid_gate * (1.0 + gate_pre * (1.0 - sigmoid_gate))).astype(jnp.bfloat16)
        grad_up_pre = (grad_gated * activated).astype(jnp.bfloat16)
        expert_dx = rounded_sum(block_terms(grad_gate_pre, gate_rows) + block_terms(grad_up_pre, up_rows))
        grad_gate_w = jnp.dot(grad_gate_pre.T, slot_x, preferred_element_type=jnp.float32).astype(jnp.bfloat16)
        grad_up_w = jnp.dot(grad_up_pre.T, slot_x, preferred_element_type=jnp.float32).astype(jnp.bfloat16)
        grad_down_w = jnp.dot(gated.T, scaled, preferred_element_type=jnp.float32).astype(jnp.bfloat16)
        return expert_out, expert_dx, grad_gate_w, grad_up_w, grad_down_w

    results = lax.map(one_expert, jnp.arange(EXPERTS, dtype=jnp.int32))
    flat_slots = slot_table.reshape(EXPERTS * group_rows)
    pair_out = jnp.zeros((pair_count + 1, D), jnp.float32).at[flat_slots].add(results[0].reshape(EXPERTS * group_rows, D))[:pair_count]
    pair_dx = jnp.zeros((pair_count + 1, D), jnp.float32).at[flat_slots].add(results[1].reshape(EXPERTS * group_rows, D))[:pair_count]
    pair_out = pair_out.reshape(TOKENS, ROUTED, D)
    mixed = jnp.sum(probs.astype(jnp.float32)[:, :, None] * pair_out, axis=1).astype(jnp.bfloat16)
    grad_probs = jnp.sum(cotangent.astype(jnp.float32)[:, None, :] * pair_out, axis=2)
    grad_hidden = jnp.sum(pair_dx.reshape(TOKENS, ROUTED, D), axis=1).astype(jnp.bfloat16)
    grad_w_gate = results[2].reshape(EXPERTS * FF, D)
    grad_w_up = results[3].reshape(EXPERTS * FF, D)
    grad_w_down = results[4].reshape(EXPERTS * FF, D)
    return (mixed, grad_hidden, grad_probs, grad_w_gate, grad_w_up, grad_w_down)
```

```python
import functools

import jax
import jax.numpy as jnp
from jax import lax
from jax.experimental import pallas as pl
from jax.experimental.pallas import tpu as pltpu
from jax.sharding import Mesh, PartitionSpec as P

EXPERTS = 32
CAP = 5
LANES = 128
TILE = 16
F32 = jnp.float32
BF16 = jnp.bfloat16
VMEM_LIMIT = 48 * 1024 * 1024


def dot(a, b, contract=((1,), (0,))):
    return lax.dot_general(a, b, (contract, ((), ())), preferred_element_type=F32)


def kernel_call(body, out_shape, flops, moved, scalars=0):
    def call(*args):
        specs = [pl.BlockSpec(memory_space=pltpu.SMEM)] * scalars
        specs += [pl.BlockSpec(memory_space=pltpu.VMEM)] * (len(args) - scalars)
        return pl.pallas_call(
            body,
            out_shape=out_shape,
            in_specs=specs,
            out_specs=jax.tree.map(lambda _: pl.BlockSpec(memory_space=pltpu.VMEM), out_shape),
            compiler_params=pltpu.CompilerParams(vmem_limit_bytes=VMEM_LIMIT),
            cost_estimate=pl.CostEstimate(flops=flops, bytes_accessed=moved, transcendentals=0),
        )(*args)

    return call


def exchange_matrix():
    n = TILE * TILE
    out_row = lax.broadcasted_iota(jnp.int32, (n, n), 0)
    in_row = lax.broadcasted_iota(jnp.int32, (n, n), 1)
    return (in_row == (out_row % TILE) * TILE + out_row // TILE).astype(BF16)


def pack_rows(left, right, packed_ref):
    swap = exchange_matrix()
    for group in range(packed_ref.shape[0] // (TILE * TILE)):
        parts = [side(group * TILE, j * LANES) for side in (left, right) for j in range(8)]
        rows = dot(swap, jnp.concatenate(parts, axis=0)).astype(BF16)
        packed_ref[pl.ds(group * TILE * TILE, TILE * TILE), :] = rows


def unpack_rows(packed_ref, left_ref, right_ref):
    swap = exchange_matrix()
    for group in range(packed_ref.shape[0] // (TILE * TILE)):
        rows = dot(swap, packed_ref[pl.ds(group * TILE * TILE, TILE * TILE), :]).astype(BF16)
        for at, side in enumerate((left_ref, right_ref)):
            for j in range(8):
                q = at * 8 + j
                side[pl.ds(group * TILE, TILE), pl.ds(j * LANES, LANES)] = rows[
                    q * TILE : (q + 1) * TILE
                ]


def token_slots(ids_row):
    tokens = ids_row.shape[1]
    expert = lax.broadcasted_iota(jnp.int32, (EXPERTS, tokens), 0)
    onehot = (expert == ids_row).astype(F32)
    before = lax.broadcasted_iota(jnp.int32, (tokens, tokens), 0)
    token = lax.broadcasted_iota(jnp.int32, (tokens, tokens), 1)
    earlier = (before < token).astype(BF16)
    counts = dot(onehot.astype(BF16), earlier)
    rank = jnp.sum(counts * onehot, axis=0, keepdims=True)
    return ids_row * CAP + rank.astype(jnp.int32)


def placement(ids_row):
    tokens = ids_row.shape[1]
    slot = lax.broadcasted_iota(jnp.int32, (EXPERTS * CAP, tokens), 0)
    return (slot == token_slots(ids_row)).astype(BF16)


def send_kernel(ids_ref, probs_ref, hidden_ref, cotangent_ref, packed_ref, placed_x, placed_s):
    select = placement(ids_ref[...])
    placed_x[...] = dot(select, hidden_ref[...]).astype(BF16)
    scaled = (probs_ref[...].astype(F32) * cotangent_ref[...].astype(F32)).astype(BF16)
    placed_s[...] = dot(select, scaled).astype(BF16)

    def side(ref):
        return lambda row, column: ref[pl.ds(row, TILE), pl.ds(column, LANES)]

    pack_rows(side(placed_x), side(placed_s), packed_ref)


def send(ids_row, probs, hidden, cotangent):
    slots = EXPERTS * CAP
    width = hidden.shape[1]
    return pl.pallas_call(
        send_kernel,
        out_shape=jax.ShapeDtypeStruct((slots * TILE, LANES), BF16),
        scratch_shapes=[pltpu.VMEM((slots, width), BF16), pltpu.VMEM((slots, width), BF16)],
        compiler_params=pltpu.CompilerParams(vmem_limit_bytes=VMEM_LIMIT),
    )(ids_row, probs, hidden, cotangent)


def unpack_kernel(packed_ref, x_ref, s_ref):
    unpack_rows(packed_ref, x_ref, s_ref)


def unpack(packed):
    slots = packed.shape[0] // TILE
    out = jax.ShapeDtypeStruct((slots, 8 * LANES), BF16)
    return kernel_call(unpack_kernel, (out, out), 2 * slots * TILE * 256 * LANES, 4 * slots * 1024 * 4)(packed)


def columns(ref, mp, step, parts):
    width = ref.shape[1] // parts
    start = pl.multiple_of(lax.rem(mp + step, parts) * width, width)
    return pl.ds(start, width)


def both(own, other):
    return jnp.concatenate([own[...], other[...]], axis=0)


def forward_kernel(parts, mp_ref, *refs):
    own, other = refs[:parts], refs[parts : 2 * parts]
    wg, wu, wd = refs[2 * parts : 2 * parts + 3]
    gate_ref, up_ref, gated_ref = refs[2 * parts + 3 : 2 * parts + 6]
    out_own, out_other = refs[2 * parts + 6 : 3 * parts + 6], refs[3 * parts + 6 :]
    mp = mp_ref[0]
    half = own[0].shape[0]
    gate = jnp.zeros((2 * half, wg.shape[0]), F32)
    up = jnp.zeros((2 * half, wg.shape[0]), F32)
    for step in range(parts):
        at = columns(wg, mp, step, parts)
        x = both(own[step], other[step])
        gate = gate + dot(x, wg[:, at], ((1,), (1,)))
        up = up + dot(x, wu[:, at], ((1,), (1,)))
    gate_ref[...] = gate
    up_ref[...] = up
    gated = (gate * (1.0 / (1.0 + jnp.exp(-gate))) * up).astype(BF16)
    gated_ref[...] = gated
    for step in range(parts):
        out = dot(gated, wd[:, columns(wd, mp, step, parts)]).astype(BF16)
        out_own[step][...] = out[:half]
        out_other[step][...] = out[half:]


def backward_kernel(parts, mp_ref, *refs):
    own, other = refs[:parts], refs[parts : 2 * parts]
    wg, wu, wd, gate_ref, up_ref = refs[2 * parts : 2 * parts + 5]
    ggp_ref, gup_ref = refs[2 * parts + 5 : 2 * parts + 7]
    dx_own, dx_other = refs[2 * parts + 7 : 3 * parts + 7], refs[3 * parts + 7 :]
    mp = mp_ref[0]
    half = own[0].shape[0]
    grad = jnp.zeros(gate_ref.shape, F32)
    for step in range(parts):
        at = columns(wd, mp, step, parts)
        grad = grad + dot(both(own[step], other[step]), wd[:, at], ((1,), (1,)))
    gate = gate_ref[...]
    sigmoid = 1.0 / (1.0 + jnp.exp(-gate))
    ggp = (grad * up_ref[...] * sigmoid * (1.0 + gate * (1.0 - sigmoid))).astype(BF16)
    gup = (grad * (gate * sigmoid)).astype(BF16)
    ggp_ref[...] = ggp
    gup_ref[...] = gup
    for step in range(parts):
        at = columns(wg, mp, step, parts)
        dx = (dot(ggp, wg[:, at]) + dot(gup, wu[:, at])).astype(BF16)
        dx_own[step][...] = dx[:half]
        dx_other[step][...] = dx[half:]


def weights_kernel(parts, mp_ref, *refs):
    x_own, x_other = refs[:parts], refs[parts : 2 * parts]
    s_own, s_other = refs[2 * parts : 3 * parts], refs[3 * parts : 4 * parts]
    ggp_ref, gup_ref, gated_ref, gwg, gwu, gwd = refs[4 * parts :]
    mp = mp_ref[0]
    rows = ((0,), (0,))
    for step in range(parts):
        at = columns(gwg, mp, step, parts)
        x = both(x_own[step], x_other[step])
        gwg[:, at] = dot(ggp_ref[...], x, rows).astype(BF16)
        gwu[:, at] = dot(gup_ref[...], x, rows).astype(BF16)
        gwd[:, at] = dot(gated_ref[...], both(s_own[step], s_other[step]), rows).astype(BF16)


def return_kernel(parts, *refs):
    out, dx, packed_ref, sum_out, sum_dx = refs[:parts], refs[parts : 2 * parts], *refs[2 * parts :]
    for terms, total in ((out, sum_out), (dx, sum_dx)):
        value = terms[0][...].astype(F32)
        for term in terms[1:]:
            value = value + term[...].astype(F32)
        total[...] = value.astype(BF16)

    def side(ref):
        return lambda row, column: ref[pl.ds(row, TILE), pl.ds(column, LANES)]

    pack_rows(side(sum_out), side(sum_dx), packed_ref)


def pack_return(out, dx):
    slots, width = out[0].shape
    return pl.pallas_call(
        functools.partial(return_kernel, len(out)),
        out_shape=jax.ShapeDtypeStruct((slots * TILE, LANES), BF16),
        scratch_shapes=[pltpu.VMEM((slots, width), BF16), pltpu.VMEM((slots, width), BF16)],
        compiler_params=pltpu.CompilerParams(vmem_limit_bytes=VMEM_LIMIT),
    )(*out, *dx)


def home_kernel(ids_ref, probs_ref, cotangent_ref, packed_ref, mixed_ref, hidden_ref, terms_ref, out_ref, dx_ref):
    select = placement(ids_ref[...])
    unpack_rows(packed_ref, out_ref, dx_ref)
    rows = ((0,), (0,))
    out = dot(select, out_ref[...], rows)
    mixed_ref[...] = (probs_ref[...].astype(F32) * out).astype(BF16)
    hidden_ref[...] = dot(select, dx_ref[...], rows).astype(BF16)
    terms_ref[...] = jnp.sum(cotangent_ref[...].astype(F32) * out, axis=1, keepdims=True)


def home(ids_row, probs, cotangent, packed):
    slots = EXPERTS * CAP
    tokens, width = cotangent.shape
    wide = jax.ShapeDtypeStruct((tokens, width), BF16)
    return pl.pallas_call(
        home_kernel,
        out_shape=(wide, wide, jax.ShapeDtypeStruct((tokens, 1), F32)),
        scratch_shapes=[pltpu.VMEM((slots, width), BF16), pltpu.VMEM((slots, width), BF16)],
        compiler_params=pltpu.CompilerParams(vmem_limit_bytes=VMEM_LIMIT),
    )(ids_row, probs, cotangent, packed)


def shift(value, axis, step):
    count = lax.axis_size(axis)
    return lax.ppermute(value, axis, [(i, (i + step) % count) for i in range(count)])


def over_yz(packed):
    parts = lax.axis_size("y") * lax.axis_size("z")
    split = packed.reshape(parts, packed.shape[0] // parts, packed.shape[1])
    return lax.all_to_all(split, ("y", "z"), 0, 0, tiled=True).reshape(packed.shape)


def body(hidden_states, expert_ids, probs, cotangent, w_gate, w_up, w_down):
    parts = lax.axis_size("mp")
    mp = lax.axis_index("mp").astype(jnp.int32).reshape(1)
    tokens = hidden_states.shape[0]
    hidden_rows, model_width = w_gate.shape
    ids_row = expert_ids.reshape(1, tokens)
    packed = over_yz(send(ids_row, probs, hidden_states, cotangent))
    x, s = unpack(packed)

    def gathered(own):
        held = [None] * parts
        held[0] = own
        for step in (1, 3, 2):
            held[step] = shift(own, "mp", -step)
        return held, [shift(part, "core", 1) for part in held]

    x_own, x_other = gathered(x)
    s_own, s_other = gathered(s)
    slots, width = x.shape
    pair = 2 * slots
    act = jax.ShapeDtypeStruct((pair, hidden_rows), F32)
    act16 = jax.ShapeDtypeStruct((pair, hidden_rows), BF16)
    part = jax.ShapeDtypeStruct((slots, width), BF16)
    weight = jax.ShapeDtypeStruct(w_gate.shape, BF16)
    product = 2 * pair * hidden_rows * model_width
    moved = 2 * hidden_rows * model_width
    gate, up, gated, *out = kernel_call(
        functools.partial(forward_kernel, parts), (act, act, act16) + (part,) * (2 * parts), 3 * product, 6 * moved, 1
    )(mp, *x_own, *x_other, w_gate, w_up, w_down)
    ggp, gup, *dx = kernel_call(
        functools.partial(backward_kernel, parts), (act16, act16) + (part,) * (2 * parts), 3 * product, 6 * moved, 1
    )(mp, *s_own, *s_other, w_gate, w_up, w_down, gate, up)
    grads = kernel_call(
        functools.partial(weights_kernel, parts), (weight, weight, weight), 3 * product, 6 * moved, 1
    )(mp, *x_own, *x_other, *s_own, *s_other, ggp, gup, gated)

    def summed(terms):
        mine, others = terms[:parts], terms[parts:]
        total = []
        for step in range(parts):
            came = shift(others[step], "core", 1)
            total.append((mine[step].astype(F32) + came.astype(F32)).astype(BF16))
        return [total[0]] + [shift(total[step], "mp", step) for step in range(1, parts)]

    back = over_yz(pack_return(summed(out), summed(dx)))
    mixed, grad_hidden, terms = home(ids_row, probs, cotangent, back)
    grad_probs = lax.psum(terms, "mp")
    return (mixed, grad_hidden, grad_probs, *grads)


def solution(mesh):
    yz_core = mesh.devices.shape[0]
    cores = 2
    columns_count = EXPERTS
    rows_y = 4
    grid = Mesh(
        mesh.devices.reshape(rows_y, yz_core // (cores * rows_y), cores, mesh.devices.shape[1]),
        ("y", "z", "core", "mp"),
    )
    assert yz_core == columns_count * cores
    blk = ("y", "z", "core")
    wide, thin, weight = P(blk, "mp"), P(blk, None), P(blk + ("mp",), None)
    return jax.shard_map(
        body,
        mesh=grid,
        in_specs=(wide, thin, thin, wide, weight, weight, weight),
        out_specs=(wide, wide, thin, weight, weight, weight),
        check_vma=False,
    )
```

```python
import functools

import jax
import jax.numpy as jnp
from jax import lax
from jax.experimental import pallas as pl
from jax.experimental.pallas import tpu as pltpu
from jax.sharding import Mesh, PartitionSpec as P

EXPERTS = 32
CAP = 5
LANES = 128
TILE = 16
F32 = jnp.float32
BF16 = jnp.bfloat16
VMEM_LIMIT = 12 * 1024 * 1024
SEND_LIMIT = 56 * 1024 * 1024


def dot(a, b, contract=((1,), (0,))):
    return lax.dot_general(a, b, (contract, ((), ())), preferred_element_type=F32)


def kernel_call(body, out_shape, flops, moved):
    def call(*args):
        specs = [pl.BlockSpec(memory_space=pltpu.VMEM)] * len(args)
        return pl.pallas_call(
            body,
            name=getattr(body, "func", body).__name__,
            out_shape=out_shape,
            in_specs=specs,
            out_specs=jax.tree.map(lambda _: pl.BlockSpec(memory_space=pltpu.VMEM), out_shape),
            compiler_params=pltpu.CompilerParams(vmem_limit_bytes=VMEM_LIMIT),
            cost_estimate=pl.CostEstimate(flops=flops, bytes_accessed=moved, transcendentals=0),
        )(*args)

    return call


def exchange_matrix():
    n = TILE * TILE
    out_row = lax.broadcasted_iota(jnp.int32, (n, n), 0)
    in_row = lax.broadcasted_iota(jnp.int32, (n, n), 1)
    return (in_row == (out_row % TILE) * TILE + out_row // TILE).astype(BF16)


def pack_rows(left, right, packed_ref):
    swap = exchange_matrix()
    rows = TILE * TILE
    for group in range(packed_ref.shape[0] // rows):
        parts = [side[group * TILE : (group + 1) * TILE] for side in (left, right)]
        stacked = [part[:, j * LANES : (j + 1) * LANES] for part in parts for j in range(TILE // 2)]
        packed_ref[pl.ds(group * rows, rows), :] = dot(swap, jnp.concatenate(stacked, axis=0)).astype(BF16)


def unpack_rows(packed_ref, wide_refs):
    swap = exchange_matrix()
    rows = TILE * TILE
    for group in range(packed_ref.shape[0] // rows):
        value = dot(swap, packed_ref[pl.ds(group * rows, rows), :]).astype(BF16)
        for at, wide in wide_refs.items():
            for j in range(TILE // 2):
                q = (at * (TILE // 2) + j) * TILE
                wide[pl.ds(group * TILE, TILE), pl.ds(j * LANES, LANES)] = value[q : q + TILE]


def token_slots(ids_row):
    tokens = ids_row.shape[1]
    expert = lax.broadcasted_iota(jnp.int32, (EXPERTS, tokens), 0)
    onehot = (expert == ids_row).astype(F32)
    before = lax.broadcasted_iota(jnp.int32, (tokens, tokens), 0)
    token = lax.broadcasted_iota(jnp.int32, (tokens, tokens), 1)
    earlier = (before < token).astype(BF16)
    counts = dot(onehot.astype(BF16), earlier)
    rank = jnp.sum(counts * onehot, axis=0, keepdims=True)
    return ids_row * CAP + rank.astype(jnp.int32)


def placement(ids_row):
    tokens = ids_row.shape[1]
    slot = lax.broadcasted_iota(jnp.int32, (EXPERTS * CAP, tokens), 0)
    return (slot == token_slots(ids_row)).astype(BF16)


def column(row):
    return jnp.transpose(jnp.broadcast_to(row.astype(F32), (LANES, row.shape[1])))[:, :1]


def column(row):
    return jnp.transpose(jnp.broadcast_to(row.astype(F32), (LANES, row.shape[1])))[:, :1]


def send_kernel(ids_hbm, probs_hbm, hidden_hbm, cotangent_hbm, packed_ref, ids, probs, hidden, cotangent, sems):
    pairs = ((ids_hbm, ids), (probs_hbm, probs), (hidden_hbm, hidden), (cotangent_hbm, cotangent))
    copies = [pltpu.make_async_copy(*pair, sems.at[at]) for at, pair in enumerate(pairs)]
    for copy in copies:
        copy.start()
    copies[0].wait()
    select = placement(ids[...])
    copies[2].wait()
    left = dot(select, hidden[...]).astype(BF16)
    copies[1].wait()
    copies[3].wait()
    scaled = (column(probs[...]) * cotangent[...].astype(F32)).astype(BF16)
    pack_rows(left, dot(select, scaled).astype(BF16), packed_ref)


def send(*args):
    return pl.pallas_call(
        send_kernel,
        name="send",
        out_shape=jax.ShapeDtypeStruct((EXPERTS * CAP * TILE, LANES), BF16),
        in_specs=[pl.BlockSpec(memory_space=pltpu.HBM)] * len(args),
        out_specs=pl.BlockSpec(memory_space=pltpu.VMEM),
        scratch_shapes=[pltpu.VMEM(a.shape, a.dtype) for a in args] + [pltpu.SemaphoreType.DMA((len(args),))],
        compiler_params=pltpu.CompilerParams(vmem_limit_bytes=SEND_LIMIT),
    )(*args)


def unpack_kernel(packed_ref, x_ref, s_ref):
    unpack_rows(packed_ref, {0: x_ref, 1: s_ref})


def unpack(packed):
    out = jax.ShapeDtypeStruct((packed.shape[0] // TILE, TILE * LANES // 2), BF16)
    return kernel_call(unpack_kernel, (out, out), 4 * packed.size * LANES, 8 * packed.size)(packed)


def blocks(parts):
    mp, core = lax.axis_index("mp"), lax.axis_index("core")
    ahead = 1 + (parts - 2) * core
    return [lax.rem(mp + step, parts) for step in (0, parts - ahead, ahead, parts // 2)]


def columns(ref, block, parts):
    width = ref.shape[1] // parts
    return pl.ds(pl.multiple_of(block * width, width), width)


def held_shards(refs):
    return [jnp.concatenate([refs[at][...], refs[at + 1][...]], axis=0) for at in range(0, len(refs), 2)]


def write_shards(values, refs):
    for at, value in enumerate(values):
        half = value.shape[0] // 2
        refs[2 * at][...] = value[:half]
        refs[2 * at + 1][...] = value[half:]


def forward_kernel(parts, *refs):
    shards, (wg, wu, wd, gate_ref, up_ref, gated_ref), out = refs[:8], refs[8:14], refs[14:]
    places = blocks(parts)
    gate, up = 0.0, 0.0
    for block, x in zip(places, held_shards(shards)):
        at = columns(wg, block, parts)
        gate = gate + dot(x, wg[:, at], ((1,), (1,)))
        up = up + dot(x, wu[:, at], ((1,), (1,)))
    gate_ref[...] = gate
    up_ref[...] = up
    gated = (gate * (1.0 / (1.0 + jnp.exp(-gate))) * up).astype(BF16)
    gated_ref[...] = gated
    write_shards([dot(gated, wd[:, columns(wd, block, parts)]).astype(BF16) for block in places], out)


def backward_kernel(parts, *refs):
    shards, (wg, wu, wd, gate_ref, up_ref, ggp_ref, gup_ref), dx = refs[:8], refs[8:15], refs[15:]
    places = blocks(parts)
    grad = 0.0
    for block, s in zip(places, held_shards(shards)):
        grad = grad + dot(s, wd[:, columns(wd, block, parts)], ((1,), (1,)))
    gate = gate_ref[...]
    sigmoid = 1.0 / (1.0 + jnp.exp(-gate))
    ggp = (grad * up_ref[...] * sigmoid * (1.0 + gate * (1.0 - sigmoid))).astype(BF16)
    gup = (grad * (gate * sigmoid)).astype(BF16)
    ggp_ref[...] = ggp
    gup_ref[...] = gup
    values = []
    for block in places:
        at = columns(wg, block, parts)
        values.append((dot(ggp, wg[:, at]) + dot(gup, wu[:, at])).astype(BF16))
    write_shards(values, dx)


def weights_kernel(parts, *refs):
    x_shards, s_shards, (ggp_ref, gup_ref, gated_ref, gwg, gwu, gwd) = refs[:8], refs[8:16], refs[16:]
    rows = ((0,), (0,))
    for block, x, s in zip(blocks(parts), held_shards(x_shards), held_shards(s_shards)):
        at = columns(gwg, block, parts)
        gwg[:, at] = dot(ggp_ref[...], x, rows).astype(BF16)
        gwu[:, at] = dot(gup_ref[...], x, rows).astype(BF16)
        gwd[:, at] = dot(gated_ref[...], s, rows).astype(BF16)


def add(*terms):
    value = terms[0].astype(F32)
    for term in terms[1:]:
        value = value + term.astype(F32)
    return value.astype(BF16)


def return_kernel(*refs):
    sums = []
    for terms in (refs[:3], refs[3:6]):
        sums.append(add(*(term[...] for term in terms)))
    pack_rows(*sums, refs[6])


def pack_return(*terms):
    packed = jax.ShapeDtypeStruct((2 * terms[0].size // LANES, LANES), BF16)
    return kernel_call(return_kernel, packed, 4 * packed.size * LANES, 8 * packed.size)(*terms)


def home_terms_kernel(ids_ref, cotangent_ref, packed_ref, terms_ref, out_ref, wide):
    unpack_rows(packed_ref, {0: wide})
    out = dot(placement(ids_ref[...]), wide[...], ((0,), (0,)))
    out_ref[...] = out
    terms = jnp.sum(cotangent_ref[...].astype(F32) * out, axis=1, keepdims=True)
    terms_ref[...] = jnp.transpose(jnp.broadcast_to(terms, (terms.shape[0], LANES)))[:1]


def home_rest_kernel(ids_ref, probs_ref, out_ref, packed_ref, mixed_ref, hidden_ref, wide):
    mixed_ref[...] = (column(probs_ref[...]) * out_ref[...]).astype(BF16)
    unpack_rows(packed_ref, {1: wide})
    hidden_ref[...] = dot(placement(ids_ref[...]), wide[...], ((0,), (0,))).astype(BF16)


def home(body, name, out_shape, *args):
    packed = args[-1]
    return pl.pallas_call(
        body,
        name=name,
        out_shape=out_shape,
        in_specs=[pl.BlockSpec(memory_space=pltpu.VMEM)] * len(args),
        scratch_shapes=[pltpu.VMEM((packed.shape[0] // TILE, TILE * LANES // 2), BF16)],
        compiler_params=pltpu.CompilerParams(vmem_limit_bytes=VMEM_LIMIT),
    )(*args)


def shift(value, axis, step):
    count = lax.axis_size(axis)
    return lax.ppermute(value, axis, [(i, (i + step) % count) for i in range(count)])


def swap_cores(value):
    return shift(value, "core", 1)


def ring(value):
    count = lax.axis_size("mp")
    pairs = [(i, (i + 1) % count) for i in range(count)]
    pairs += [(count + i, count + (i - 1) % count) for i in range(count)]
    return lax.ppermute(value, ("core", "mp"), pairs)


def after(value, *first):
    return lax.optimization_barrier((value, *first))[0]


def summed(own, own_other, behind, behind_other, ahead, ahead_other, opposite, opposite_other):
    tail = ring(add(opposite, swap_cores(opposite_other)))
    came_other = ring(add(ahead_other, swap_cores(behind)))
    came = ring(add(ahead, swap_cores(behind_other), tail))
    return own, came, swap_cores(add(own_other, came_other))


def over_yz(packed):
    parts = lax.axis_size("y") * lax.axis_size("z")
    split = packed.reshape(parts, packed.shape[0] // parts, packed.shape[1])
    return lax.all_to_all(split, ("y", "z"), 0, 0, tiled=True).reshape(packed.shape)


def body(hidden_states, expert_ids, probs, cotangent, w_gate, w_up, w_down):
    parts = lax.axis_size("mp")
    tokens = hidden_states.shape[0]
    hidden_rows, model_width = w_gate.shape
    ids_row, probs_row = expert_ids.reshape(1, tokens), probs.reshape(1, tokens)
    x_own, s_own = unpack(over_yz(send(ids_row, probs_row, hidden_states, cotangent)))
    x_other, s_other = swap_cores(x_own), swap_cores(s_own)
    x_behind = ring(x_own)
    x_behind_other = ring(x_other)
    x_opposite = ring(x_behind)
    x_shards = (x_own, x_other, x_behind, x_behind_other)
    x_shards += (swap_cores(x_behind_other), swap_cores(x_behind), x_opposite, swap_cores(x_opposite))
    slots, width = x_own.shape
    pair = 2 * slots
    act = jax.ShapeDtypeStruct((pair, hidden_rows), F32)
    act16 = jax.ShapeDtypeStruct((pair, hidden_rows), BF16)
    sums = (jax.ShapeDtypeStruct((slots, width), BF16),) * (2 * parts)
    weight = jax.ShapeDtypeStruct(w_gate.shape, BF16)
    product = 2 * pair * hidden_rows * model_width
    moved = 2 * hidden_rows * model_width
    gate, up, gated, *out = kernel_call(
        functools.partial(forward_kernel, parts), (act, act, act16) + sums, 3 * product, 6 * moved
    )(*x_shards, w_gate, w_up, w_down)
    s_behind = ring(s_own)
    s_behind_other = ring(after(s_other, x_behind))
    s_opposite = ring(s_behind)
    s_shards = (s_own, s_other, s_behind, s_behind_other)
    s_shards += tuple(
        swap_cores(after(value, gate)) for value in (s_behind_other, s_behind, s_opposite)
    )
    s_shards = s_shards[:6] + (s_opposite, s_shards[6])
    ggp, gup, *dx = kernel_call(
        functools.partial(backward_kernel, parts), (act16, act16) + sums, 3 * product, 6 * moved
    )(*s_shards, w_gate, w_up, w_down, gate, up)
    out_sum = summed(*out)
    own, own_other, behind, behind_other, ahead, ahead_other, opposite, opposite_other = dx
    tail = ring(add(opposite, swap_cores(opposite_other)))
    came_other = ring(add(ahead_other, swap_cores(behind)))
    last = add(ahead, swap_cores(behind_other), tail)
    came = ring(last)
    grads = kernel_call(functools.partial(weights_kernel, parts), (weight, weight, weight), 3 * product, 6 * moved)(
        *x_shards, *s_shards, after(ggp, last), gup, gated
    )
    dx_sum = (own, after(came, grads[0]), swap_cores(add(own_other, came_other)))
    packed = over_yz(pack_return(*out_sum, *dx_sum))
    wide = jax.ShapeDtypeStruct(hidden_states.shape, BF16)
    row = jax.ShapeDtypeStruct((1, tokens), F32)
    placed = jax.ShapeDtypeStruct(hidden_states.shape, F32)
    terms, out_rows = home(home_terms_kernel, "home_terms", (row, placed), ids_row, cotangent, packed)
    one, two, three = (shift(terms, "mp", step) for step in range(1, parts))
    mixed, grad_hidden = home(home_rest_kernel, "home_rest", (wide, wide), ids_row, probs_row, out_rows, packed)
    grad_probs = ((terms + two) + (one + three)).reshape(tokens, 1)
    return (mixed, grad_hidden, grad_probs, *grads)


def solution(mesh):
    yz_core = mesh.devices.shape[0]
    cores = 2
    columns_count = EXPERTS
    rows_y = 4
    grid = Mesh(
        mesh.devices.reshape(rows_y, yz_core // (cores * rows_y), cores, mesh.devices.shape[1]),
        ("y", "z", "core", "mp"),
    )
    assert yz_core == columns_count * cores
    blk = ("y", "z", "core")
    wide, thin, weight = P(blk, "mp"), P(blk, None), P(blk + ("mp",), None)
    return jax.shard_map(
        body,
        mesh=grid,
        in_specs=(wide, thin, thin, wide, weight, weight, weight),
        out_specs=(wide, wide, thin, weight, weight, weight),
        check_vma=False,
    )
```

```python
import functools

import jax
import jax.numpy as jnp
from jax import lax
from jax.experimental import pallas as pl
from jax.experimental.pallas import tpu as pltpu
from jax.sharding import Mesh, PartitionSpec as P

EXPERTS = 32
CAP = 5
LANES = 128
TILE = 16
F32 = jnp.float32
BF16 = jnp.bfloat16
VMEM_LIMIT = 12 * 1024 * 1024
SEND_LIMIT = 56 * 1024 * 1024


def dot(a, b, contract=((1,), (0,))):
    return lax.dot_general(a, b, (contract, ((), ())), preferred_element_type=F32)


def kernel_call(body, out_shape, flops, moved):
    def call(*args):
        specs = [pl.BlockSpec(memory_space=pltpu.VMEM)] * len(args)
        return pl.pallas_call(
            body,
            name=getattr(body, "func", body).__name__,
            out_shape=out_shape,
            in_specs=specs,
            out_specs=jax.tree.map(lambda _: pl.BlockSpec(memory_space=pltpu.VMEM), out_shape),
            compiler_params=pltpu.CompilerParams(vmem_limit_bytes=VMEM_LIMIT),
            cost_estimate=pl.CostEstimate(flops=flops, bytes_accessed=moved, transcendentals=0),
        )(*args)

    return call


def exchange_matrix():
    n = TILE * TILE
    out_row = lax.broadcasted_iota(jnp.int32, (n, n), 0)
    in_row = lax.broadcasted_iota(jnp.int32, (n, n), 1)
    return (in_row == (out_row % TILE) * TILE + out_row // TILE).astype(BF16)


def pack_rows(left, right, packed_ref):
    swap = exchange_matrix()
    rows = TILE * TILE
    for group in range(packed_ref.shape[0] // rows):
        parts = [side[group * TILE : (group + 1) * TILE] for side in (left, right)]
        stacked = [part[:, j * LANES : (j + 1) * LANES] for part in parts for j in range(TILE // 2)]
        packed_ref[pl.ds(group * rows, rows), :] = dot(swap, jnp.concatenate(stacked, axis=0)).astype(BF16)


def unpack_rows(packed_ref, wide_refs):
    swap = exchange_matrix()
    rows = TILE * TILE
    for group in range(packed_ref.shape[0] // rows):
        value = dot(swap, packed_ref[pl.ds(group * rows, rows), :]).astype(BF16)
        for at, wide in wide_refs.items():
            for j in range(TILE // 2):
                q = (at * (TILE // 2) + j) * TILE
                wide[pl.ds(group * TILE, TILE), pl.ds(j * LANES, LANES)] = value[q : q + TILE]


def token_slots(ids_row):
    tokens = ids_row.shape[1]
    expert = lax.broadcasted_iota(jnp.int32, (EXPERTS, tokens), 0)
    onehot = (expert == ids_row).astype(F32)
    before = lax.broadcasted_iota(jnp.int32, (tokens, tokens), 0)
    token = lax.broadcasted_iota(jnp.int32, (tokens, tokens), 1)
    earlier = (before < token).astype(BF16)
    counts = dot(onehot.astype(BF16), earlier)
    rank = jnp.sum(counts * onehot, axis=0, keepdims=True)
    return ids_row * CAP + rank.astype(jnp.int32)


def placement(ids_row):
    tokens = ids_row.shape[1]
    slot = lax.broadcasted_iota(jnp.int32, (EXPERTS * CAP, tokens), 0)
    return (slot == token_slots(ids_row)).astype(BF16)


def column(row):
    return jnp.transpose(jnp.broadcast_to(row.astype(F32), (LANES, row.shape[1])))[:, :1]


def column(row):
    return jnp.transpose(jnp.broadcast_to(row.astype(F32), (LANES, row.shape[1])))[:, :1]


def send_kernel(ids_hbm, probs_hbm, hidden_hbm, cotangent_hbm, packed_ref, ids, probs, hidden, cotangent, sems):
    pairs = ((ids_hbm, ids), (probs_hbm, probs), (hidden_hbm, hidden), (cotangent_hbm, cotangent))
    copies = [pltpu.make_async_copy(*pair, sems.at[at]) for at, pair in enumerate(pairs)]
    for copy in copies:
        copy.start()
    copies[0].wait()
    select = placement(ids[...])
    copies[2].wait()
    left = dot(select, hidden[...]).astype(BF16)
    copies[1].wait()
    copies[3].wait()
    scaled = (column(probs[...]) * cotangent[...].astype(F32)).astype(BF16)
    pack_rows(left, dot(select, scaled).astype(BF16), packed_ref)


def send(*args):
    return pl.pallas_call(
        send_kernel,
        name="send",
        out_shape=jax.ShapeDtypeStruct((EXPERTS * CAP * TILE, LANES), BF16),
        in_specs=[pl.BlockSpec(memory_space=pltpu.HBM)] * len(args),
        out_specs=pl.BlockSpec(memory_space=pltpu.VMEM),
        scratch_shapes=[pltpu.VMEM(a.shape, a.dtype) for a in args] + [pltpu.SemaphoreType.DMA((len(args),))],
        compiler_params=pltpu.CompilerParams(vmem_limit_bytes=SEND_LIMIT),
    )(*args)


def unpack_kernel(packed_ref, x_ref, s_ref):
    unpack_rows(packed_ref, {0: x_ref, 1: s_ref})


def unpack(packed):
    out = jax.ShapeDtypeStruct((packed.shape[0] // TILE, TILE * LANES // 2), BF16)
    return kernel_call(unpack_kernel, (out, out), 4 * packed.size * LANES, 8 * packed.size)(packed)


def blocks(parts):
    mp, core = lax.axis_index("mp"), lax.axis_index("core")
    ahead = 1 + (parts - 2) * core
    return [lax.rem(mp + step, parts) for step in (0, parts - ahead, ahead, parts // 2)]


def columns(ref, block, parts):
    width = ref.shape[1] // parts
    return pl.ds(pl.multiple_of(block * width, width), width)


def held(own, other):
    return jnp.concatenate([own[...], other[...]], axis=0)


def write_shards(values, refs):
    for at, value in enumerate(values):
        half = value.shape[0] // 2
        refs[2 * at][...] = value[:half]
        refs[2 * at + 1][...] = value[half:]


def first_x_kernel(parts, own, own_other, behind, behind_other, wg, wu, wd, gate_ref, up_ref):
    gate, up = 0.0, 0.0
    for block, mine, other in zip(blocks(parts), (own, behind), (own_other, behind_other)):
        at = columns(wg, block, parts)
        x = held(mine, other)
        gate = gate + dot(x, wg[:, at], ((1,), (1,)))
        up = up + dot(x, wu[:, at], ((1,), (1,)))
    gate_ref[...] = gate
    up_ref[...] = up


def first_s_kernel(parts, own, own_other, behind, behind_other, wd, grad_ref):
    grad = 0.0
    for block, mine, other in zip(blocks(parts), (own, behind), (own_other, behind_other)):
        grad = grad + dot(held(mine, other), wd[:, columns(wd, block, parts)], ((1,), (1,)))
    grad_ref[...] = grad


def forward_kernel(parts, *refs):
    shards, (wg, wu, wd, gate_in, up_in, gate_ref, up_ref, gated_ref), out = refs[:4], refs[4:12], refs[12:]
    places = blocks(parts)
    gate, up = gate_in[...], up_in[...]
    for at in range(2):
        cut = columns(wg, places[2 + at], parts)
        x = held(shards[2 * at], shards[2 * at + 1])
        gate = gate + dot(x, wg[:, cut], ((1,), (1,)))
        up = up + dot(x, wu[:, cut], ((1,), (1,)))
    gate_ref[...] = gate
    up_ref[...] = up
    gated = (gate * (1.0 / (1.0 + jnp.exp(-gate))) * up).astype(BF16)
    gated_ref[...] = gated
    write_shards([dot(gated, wd[:, columns(wd, block, parts)]).astype(BF16) for block in places], out)


def backward_kernel(parts, *refs):
    shards, (wg, wu, wd, gate_ref, up_ref, grad_in, ggp_ref, gup_ref), dx = refs[:4], refs[4:12], refs[12:]
    places = blocks(parts)
    grad = grad_in[...]
    for at in range(2):
        cut = columns(wd, places[2 + at], parts)
        grad = grad + dot(held(shards[2 * at], shards[2 * at + 1]), wd[:, cut], ((1,), (1,)))
    gate = gate_ref[...]
    sigmoid = 1.0 / (1.0 + jnp.exp(-gate))
    ggp = (grad * up_ref[...] * sigmoid * (1.0 + gate * (1.0 - sigmoid))).astype(BF16)
    gup = (grad * (gate * sigmoid)).astype(BF16)
    ggp_ref[...] = ggp
    gup_ref[...] = gup
    values = []
    for block in places:
        at = columns(wg, block, parts)
        values.append((dot(ggp, wg[:, at]) + dot(gup, wu[:, at])).astype(BF16))
    write_shards(values, dx)


def weights_kernel(parts, *refs):
    x_shards, s_shards, (ggp_ref, gup_ref, gated_ref, gwg, gwu, gwd) = refs[:8], refs[8:16], refs[16:]
    rows = ((0,), (0,))
    for step, block in enumerate(blocks(parts)):
        at = columns(gwg, block, parts)
        x, s = (held(side[2 * step], side[2 * step + 1]) for side in (x_shards, s_shards))
        gwg[:, at] = dot(ggp_ref[...], x, rows).astype(BF16)
        gwu[:, at] = dot(gup_ref[...], x, rows).astype(BF16)
        gwd[:, at] = dot(gated_ref[...], s, rows).astype(BF16)


def add(*terms):
    value = terms[0].astype(F32)
    for term in terms[1:]:
        value = value + term.astype(F32)
    return value.astype(BF16)


def return_kernel(*refs):
    sums = []
    for terms in (refs[:3], refs[3:6]):
        sums.append(add(*(term[...] for term in terms)))
    pack_rows(*sums, refs[6])


def pack_return(*terms):
    packed = jax.ShapeDtypeStruct((2 * terms[0].size // LANES, LANES), BF16)
    return kernel_call(return_kernel, packed, 4 * packed.size * LANES, 8 * packed.size)(*terms)


def home_terms_kernel(ids_ref, cotangent_ref, packed_ref, terms_ref, out_ref, wide):
    unpack_rows(packed_ref, {0: wide})
    out = dot(placement(ids_ref[...]), wide[...], ((0,), (0,)))
    out_ref[...] = out
    terms = jnp.sum(cotangent_ref[...].astype(F32) * out, axis=1, keepdims=True)
    terms_ref[...] = jnp.transpose(jnp.broadcast_to(terms, (terms.shape[0], LANES)))[:1]


def home_rest_kernel(ids_ref, probs_ref, out_ref, packed_ref, mixed_ref, hidden_ref, wide):
    mixed_ref[...] = (column(probs_ref[...]) * out_ref[...]).astype(BF16)
    unpack_rows(packed_ref, {1: wide})
    hidden_ref[...] = dot(placement(ids_ref[...]), wide[...], ((0,), (0,))).astype(BF16)


def home(body, name, out_shape, *args):
    packed = args[-1]
    return pl.pallas_call(
        body,
        name=name,
        out_shape=out_shape,
        in_specs=[pl.BlockSpec(memory_space=pltpu.VMEM)] * len(args),
        scratch_shapes=[pltpu.VMEM((packed.shape[0] // TILE, TILE * LANES // 2), BF16)],
        compiler_params=pltpu.CompilerParams(vmem_limit_bytes=VMEM_LIMIT),
    )(*args)


def shift(value, axis, step):
    count = lax.axis_size(axis)
    return lax.ppermute(value, axis, [(i, (i + step) % count) for i in range(count)])


def swap_cores(value):
    return shift(value, "core", 1)


def ring(value):
    count = lax.axis_size("mp")
    pairs = [(i, (i + 1) % count) for i in range(count)]
    pairs += [(count + i, count + (i - 1) % count) for i in range(count)]
    return lax.ppermute(value, ("core", "mp"), pairs)


def after(value, *first):
    return lax.optimization_barrier((value, *first))[0]


def ring_inputs(own, own_other, behind, behind_other, ahead, ahead_other, opposite, opposite_other):
    return add(opposite, swap_cores(opposite_other)), add(ahead_other, swap_cores(behind))


def summed(terms, tail, other):
    own, own_other, _, behind_other, ahead, *_ = terms
    came_other = ring(other)
    last = add(ahead, swap_cores(behind_other), ring(tail))
    return (own, ring(last), swap_cores(add(own_other, came_other))), last


def over_yz(packed):
    parts = lax.axis_size("y") * lax.axis_size("z")
    split = packed.reshape(parts, packed.shape[0] // parts, packed.shape[1])
    return lax.all_to_all(split, ("y", "z"), 0, 0, tiled=True).reshape(packed.shape)


def body(hidden_states, expert_ids, probs, cotangent, w_gate, w_up, w_down):
    parts = lax.axis_size("mp")
    tokens = hidden_states.shape[0]
    hidden_rows, model_width = w_gate.shape
    ids_row, probs_row = expert_ids.reshape(1, tokens), probs.reshape(1, tokens)
    x_own, s_own = unpack(over_yz(send(ids_row, probs_row, hidden_states, cotangent)))
    x_other, s_other = swap_cores(x_own), swap_cores(s_own)
    x_behind, x_behind_other = ring(x_own), ring(x_other)
    s_behind, s_behind_other = ring(s_own), ring(s_other)
    x_opposite, s_opposite = ring(x_behind), ring(s_behind)
    x_first, s_first = (x_own, x_other, x_behind, x_behind_other), (s_own, s_other, s_behind, s_behind_other)
    slots, width = x_own.shape
    pair = 2 * slots
    act = jax.ShapeDtypeStruct((pair, hidden_rows), F32)
    act16 = jax.ShapeDtypeStruct((pair, hidden_rows), BF16)
    sums = (jax.ShapeDtypeStruct((slots, width), BF16),) * (2 * parts)
    weight = jax.ShapeDtypeStruct(w_gate.shape, BF16)
    product = 2 * pair * hidden_rows * model_width
    moved = 2 * hidden_rows * model_width
    weights = (w_gate, w_up, w_down)
    waited = after(x_behind_other, s_behind)
    gate, up = kernel_call(functools.partial(first_x_kernel, parts), (act, act), product, 3 * moved)(
        *x_first[:3], waited, *weights
    )
    grad = kernel_call(functools.partial(first_s_kernel, parts), act, product // 2, moved)(*s_first, w_down)
    x_rest = (swap_cores(x_behind_other), swap_cores(x_behind), x_opposite, swap_cores(after(x_opposite, gate, grad)))
    s_rest = (swap_cores(s_behind_other), swap_cores(s_behind), s_opposite, swap_cores(after(s_opposite, grad)))
    gate, up, gated, *out = kernel_call(
        functools.partial(forward_kernel, parts), (act, act, act16) + sums, 2 * product, 5 * moved
    )(*x_rest, *weights, gate, up)
    out_tail, out_other = ring_inputs(*out)
    ggp, gup, *dx = kernel_call(
        functools.partial(backward_kernel, parts), (act16, act16) + sums, 5 * product // 2, 5 * moved
    )(*s_rest, *weights, gate, up, grad)
    out_sum, _ = summed(out, out_tail, out_other)
    dx_sum, last = summed(dx, *ring_inputs(*dx))
    grads = kernel_call(functools.partial(weights_kernel, parts), (weight, weight, weight), 3 * product, 6 * moved)(
        *x_first, *x_rest, *s_first, *s_rest, after(ggp, last), gup, gated
    )
    dx_sum = (dx_sum[0], after(dx_sum[1], grads[0]), dx_sum[2])
    packed = over_yz(pack_return(*out_sum, *dx_sum))
    wide = jax.ShapeDtypeStruct(hidden_states.shape, BF16)
    row = jax.ShapeDtypeStruct((1, tokens), F32)
    placed = jax.ShapeDtypeStruct(hidden_states.shape, F32)
    terms, out_rows = home(home_terms_kernel, "home_terms", (row, placed), ids_row, cotangent, packed)
    one, two, three = (shift(terms, "mp", step) for step in range(1, parts))
    mixed, grad_hidden = home(home_rest_kernel, "home_rest", (wide, wide), ids_row, probs_row, out_rows, packed)
    grad_probs = ((terms + two) + (one + three)).reshape(tokens, 1)
    return (mixed, grad_hidden, grad_probs, *grads)


def solution(mesh):
    yz_core = mesh.devices.shape[0]
    cores = 2
    columns_count = EXPERTS
    rows_y = 4
    grid = Mesh(
        mesh.devices.reshape(rows_y, yz_core // (cores * rows_y), cores, mesh.devices.shape[1]),
        ("y", "z", "core", "mp"),
    )
    assert yz_core == columns_count * cores
    blk = ("y", "z", "core")
    wide, thin, weight = P(blk, "mp"), P(blk, None), P(blk + ("mp",), None)
    return jax.shard_map(
        body,
        mesh=grid,
        in_specs=(wide, thin, thin, wide, weight, weight, weight),
        out_specs=(wide, wide, thin, weight, weight, weight),
        check_vma=False,
    )
```

```python
import functools

import jax
import jax.numpy as jnp
from jax import lax
from jax.experimental import pallas as pl
from jax.experimental.pallas import tpu as pltpu
from jax.sharding import Mesh, PartitionSpec as P

EXPERTS = 32
CAP = 5
ROOM = CAP + 1
LANES = 128
TILE = 16
F32 = jnp.float32
BF16 = jnp.bfloat16
VMEM_LIMIT = 12 * 1024 * 1024
SEND_LIMIT = 56 * 1024 * 1024


def dot(a, b, contract=((1,), (0,))):
    return lax.dot_general(a, b, (contract, ((), ())), preferred_element_type=F32)


def kernel_call(body, out_shape, flops, moved):
    def call(*args):
        specs = [pl.BlockSpec(memory_space=pltpu.VMEM)] * len(args)
        return pl.pallas_call(
            body,
            name=getattr(body, "func", body).__name__,
            out_shape=out_shape,
            in_specs=specs,
            out_specs=jax.tree.map(lambda _: pl.BlockSpec(memory_space=pltpu.VMEM), out_shape),
            compiler_params=pltpu.CompilerParams(vmem_limit_bytes=VMEM_LIMIT),
            cost_estimate=pl.CostEstimate(flops=flops, bytes_accessed=moved, transcendentals=0),
        )(*args)

    return call


def exchange_matrix():
    n = TILE * TILE
    out_row = lax.broadcasted_iota(jnp.int32, (n, n), 0)
    in_row = lax.broadcasted_iota(jnp.int32, (n, n), 1)
    return (in_row == (out_row % TILE) * TILE + out_row // TILE).astype(BF16)


def pack_rows(left, right, packed_ref):
    swap = exchange_matrix()
    rows = TILE * TILE
    for group in range(packed_ref.shape[0] // rows):
        parts = [side[group * TILE : (group + 1) * TILE] for side in (left, right)]
        stacked = [part[:, j * LANES : (j + 1) * LANES] for part in parts for j in range(TILE // 2)]
        packed_ref[pl.ds(group * rows, rows), :] = dot(swap, jnp.concatenate(stacked, axis=0)).astype(BF16)


def unpack_rows(packed_ref, wide_refs):
    swap = exchange_matrix()
    rows = TILE * TILE
    for group in range(packed_ref.shape[0] // rows):
        value = dot(swap, packed_ref[pl.ds(group * rows, rows), :]).astype(BF16)
        for at, wide in wide_refs.items():
            for j in range(TILE // 2):
                q = (at * (TILE // 2) + j) * TILE
                wide[pl.ds(group * TILE, TILE), pl.ds(j * LANES, LANES)] = value[q : q + TILE]


def token_ranks(ids_row):
    tokens = ids_row.shape[1]
    expert = lax.broadcasted_iota(jnp.int32, (EXPERTS, tokens), 0)
    onehot = (expert == ids_row).astype(F32)
    before = lax.broadcasted_iota(jnp.int32, (tokens, tokens), 0)
    token = lax.broadcasted_iota(jnp.int32, (tokens, tokens), 1)
    earlier = (before < token).astype(BF16)
    counts = dot(onehot.astype(BF16), earlier)
    return jnp.sum(counts * onehot, axis=0, keepdims=True).astype(jnp.int32)


def placement(ids_row, ranks, room):
    slot = lax.broadcasted_iota(jnp.int32, (EXPERTS * room, ids_row.shape[1]), 0)
    return (slot == ids_row * room + ranks).astype(BF16)


def column(row):
    return jnp.transpose(jnp.broadcast_to(row.astype(F32), (LANES, row.shape[1])))[:, :1]


def column(row):
    return jnp.transpose(jnp.broadcast_to(row.astype(F32), (LANES, row.shape[1])))[:, :1]


def send_kernel(ids_hbm, probs_hbm, hidden_hbm, cotangent_hbm, packed_ref, ids, probs, hidden, cotangent, sems):
    pairs = ((ids_hbm, ids), (probs_hbm, probs), (hidden_hbm, hidden), (cotangent_hbm, cotangent))
    copies = [pltpu.make_async_copy(*pair, sems.at[at]) for at, pair in enumerate(pairs)]
    for copy in copies:
        copy.start()
    copies[0].wait()
    select = placement(ids[...], token_ranks(ids[...]), CAP)
    copies[2].wait()
    left = dot(select, hidden[...]).astype(BF16)
    copies[1].wait()
    copies[3].wait()
    scaled = (column(probs[...]) * cotangent[...].astype(F32)).astype(BF16)
    pack_rows(left, dot(select, scaled).astype(BF16), packed_ref)


def send(*args):
    return pl.pallas_call(
        send_kernel,
        name="send",
        out_shape=jax.ShapeDtypeStruct((EXPERTS * CAP * TILE, LANES), BF16),
        in_specs=[pl.BlockSpec(memory_space=pltpu.HBM)] * len(args),
        out_specs=pl.BlockSpec(memory_space=pltpu.VMEM),
        scratch_shapes=[pltpu.VMEM(a.shape, a.dtype) for a in args] + [pltpu.SemaphoreType.DMA((len(args),))],
        compiler_params=pltpu.CompilerParams(vmem_limit_bytes=SEND_LIMIT),
    )(*args)


def unpack_kernel(packed_ref, x_ref, s_ref):
    unpack_rows(packed_ref, {0: x_ref, 1: s_ref})


def unpack(packed):
    out = jax.ShapeDtypeStruct((packed.shape[0] // TILE, TILE * LANES // 2), BF16)
    return kernel_call(unpack_kernel, (out, out), 4 * packed.size * LANES, 8 * packed.size)(packed)


def blocks(parts):
    mp, core = lax.axis_index("mp"), lax.axis_index("core")
    ahead = 1 + (parts - 2) * core
    return [lax.rem(mp + step, parts) for step in (0, parts - ahead, ahead, parts // 2)]


def columns(ref, block, parts):
    width = ref.shape[1] // parts
    return pl.ds(pl.multiple_of(block * width, width), width)


def held(own, other):
    return jnp.concatenate([own[...], other[...]], axis=0)


def write_shards(values, refs):
    for at, value in enumerate(values):
        half = value.shape[0] // 2
        refs[2 * at][...] = value[:half]
        refs[2 * at + 1][...] = value[half:]


def first_x_kernel(parts, own, own_other, behind, behind_other, wg, wu, wd, gate_ref, up_ref):
    gate, up = 0.0, 0.0
    for block, mine, other in zip(blocks(parts), (own, behind), (own_other, behind_other)):
        at = columns(wg, block, parts)
        x = held(mine, other)
        gate = gate + dot(x, wg[:, at], ((1,), (1,)))
        up = up + dot(x, wu[:, at], ((1,), (1,)))
    gate_ref[...] = gate
    up_ref[...] = up


def first_s_kernel(parts, own, own_other, behind, behind_other, wd, grad_ref):
    grad = 0.0
    for block, mine, other in zip(blocks(parts), (own, behind), (own_other, behind_other)):
        grad = grad + dot(held(mine, other), wd[:, columns(wd, block, parts)], ((1,), (1,)))
    grad_ref[...] = grad


def forward_kernel(parts, *refs):
    shards, (wg, wu, wd, gate_in, up_in, gate_ref, up_ref, gated_ref), out = refs[:4], refs[4:12], refs[12:]
    places = blocks(parts)
    gate, up = gate_in[...], up_in[...]
    for at in range(2):
        cut = columns(wg, places[2 + at], parts)
        x = held(shards[2 * at], shards[2 * at + 1])
        gate = gate + dot(x, wg[:, cut], ((1,), (1,)))
        up = up + dot(x, wu[:, cut], ((1,), (1,)))
    gate_ref[...] = gate
    up_ref[...] = up
    gated = (gate * (1.0 / (1.0 + jnp.exp(-gate))) * up).astype(BF16)
    gated_ref[...] = gated
    write_shards([dot(gated, wd[:, columns(wd, block, parts)]).astype(BF16) for block in places], out)


def backward_kernel(parts, *refs):
    shards, (wg, wu, wd, gate_ref, up_ref, gated_ref, grad_in, ggp_ref, gup_ref), dx = refs[:4], refs[4:13], refs[13:]
    places = blocks(parts)
    grad = grad_in[...]
    for at in range(2):
        cut = columns(wd, places[2 + at], parts)
        grad = grad + dot(held(shards[2 * at], shards[2 * at + 1]), wd[:, cut], ((1,), (1,)))
    terms = jnp.sum(grad * gated_ref[...].astype(F32), axis=1, keepdims=True)
    terms = jnp.broadcast_to(terms, (terms.shape[0], LANES)).astype(BF16)
    gate = gate_ref[...]
    sigmoid = 1.0 / (1.0 + jnp.exp(-gate))
    ggp = (grad * up_ref[...] * sigmoid * (1.0 + gate * (1.0 - sigmoid))).astype(BF16)
    gup = (grad * (gate * sigmoid)).astype(BF16)
    ggp_ref[...] = ggp
    gup_ref[...] = gup
    values = []
    for block in places:
        at = columns(wg, block, parts)
        value = (dot(ggp, wg[:, at]) + dot(gup, wu[:, at])).astype(BF16)
        values.append(jnp.concatenate([value, terms], axis=1))
    write_shards(values, dx)


def weights_kernel(parts, *refs):
    x_shards, s_shards, (ggp_ref, gup_ref, gated_ref, gwg, gwu, gwd) = refs[:8], refs[8:16], refs[16:]
    rows = ((0,), (0,))
    for step, block in enumerate(blocks(parts)):
        at = columns(gwg, block, parts)
        x, s = (held(side[2 * step], side[2 * step + 1]) for side in (x_shards, s_shards))
        gwg[:, at] = dot(ggp_ref[...], x, rows).astype(BF16)
        gwu[:, at] = dot(gup_ref[...], x, rows).astype(BF16)
        gwd[:, at] = dot(gated_ref[...], s, rows).astype(BF16)


def add(*terms):
    value = terms[0].astype(F32)
    for term in terms[1:]:
        value = value + term.astype(F32)
    return value.astype(BF16)


def slot_parts(shape, axis, room):
    slot = lax.broadcasted_iota(jnp.int32, shape, axis)
    expert = jnp.floor((slot.astype(F32) + 0.5) * (1.0 / room)).astype(jnp.int32)
    return expert, slot - expert * room


def return_kernel(*refs):
    out, dx, packed_ref = refs[:3], refs[3:6], refs[6]
    width = out[0].shape[1]
    slots, wide = EXPERTS * CAP, EXPERTS * ROOM
    row_expert, row_place = slot_parts((wide, slots), 0, ROOM)
    expert, place = slot_parts((wide, slots), 1, CAP)
    same = row_expert == expert
    spread = (same & (row_place == place)).astype(BF16)
    last = (same & (row_place == CAP)).astype(BF16)
    _, lane_place = slot_parts((slots, LANES), 0, CAP)
    lane = lax.broadcasted_iota(jnp.int32, (slots, LANES), 1)
    sums = add(*(term[...] for term in dx))
    terms = jnp.where(lane_place == lane, sums[:, width:].astype(F32), 0.0).astype(BF16)
    left = dot(spread, add(*(term[...] for term in out)))
    left = jnp.concatenate([left[:, :LANES] + dot(last, terms), left[:, LANES:]], axis=1)
    pack_rows(left.astype(BF16), dot(spread, sums[:, :width]).astype(BF16), packed_ref)


def home_kernel(ids_ref, probs_ref, packed_ref, mixed_ref, hidden_ref, grad_ref, out_wide, dx_wide):
    ids = ids_ref[...]
    ranks = token_ranks(ids)
    select = placement(ids, ranks, ROOM)
    unpack_rows(packed_ref, {0: out_wide, 1: dx_wide})
    rows = ((0,), (0,))
    probs = column(probs_ref[...])
    mixed_ref[...] = (probs * dot(select, out_wide[...], rows)).astype(BF16)
    hidden_ref[...] = dot(select, dx_wide[...], rows).astype(BF16)
    last = placement(ids, jnp.full_like(ranks, CAP), ROOM)
    parts = dot(last, out_wide[:, :LANES], rows)
    lane = lax.broadcasted_iota(jnp.int32, (ids.shape[1], LANES), 1)
    terms = jnp.where(lane == column(ranks).astype(jnp.int32), parts, 0.0)
    grad = jnp.sum(terms, axis=1, keepdims=True) / probs
    grad_ref[...] = jnp.transpose(jnp.broadcast_to(grad, (grad.shape[0], LANES)))[:1]


def home(ids_row, probs_row, packed):
    slots, width, tokens = packed.shape[0] // TILE, TILE * LANES // 2, ids_row.shape[1]
    wide = jax.ShapeDtypeStruct((tokens, width), BF16)
    return pl.pallas_call(
        home_kernel,
        name="home",
        out_shape=(wide, wide, jax.ShapeDtypeStruct((1, tokens), F32)),
        in_specs=[pl.BlockSpec(memory_space=pltpu.VMEM)] * 3,
        scratch_shapes=[pltpu.VMEM((slots, width), BF16)] * 2,
        compiler_params=pltpu.CompilerParams(vmem_limit_bytes=VMEM_LIMIT),
    )(ids_row, probs_row, packed)


def shift(value, axis, step):
    count = lax.axis_size(axis)
    return lax.ppermute(value, axis, [(i, (i + step) % count) for i in range(count)])


def swap_cores(value):
    return shift(value, "core", 1)


def ring(value):
    count = lax.axis_size("mp")
    pairs = [(i, (i + 1) % count) for i in range(count)]
    pairs += [(count + i, count + (i - 1) % count) for i in range(count)]
    return lax.ppermute(value, ("core", "mp"), pairs)


def after(value, *first):
    return lax.optimization_barrier((value, *first))[0]


def ring_inputs(own, own_other, behind, behind_other, ahead, ahead_other, opposite, opposite_other):
    return add(opposite, swap_cores(opposite_other)), add(ahead_other, swap_cores(behind))


def summed(terms, tail, other):
    own, own_other, _, behind_other, ahead, *_ = terms
    came_other = ring(other)
    last = add(ahead, swap_cores(behind_other), ring(tail))
    return (own, ring(last), swap_cores(add(own_other, came_other))), last


def over_yz(packed):
    parts = lax.axis_size("y") * lax.axis_size("z")
    split = packed.reshape(parts, packed.shape[0] // parts, packed.shape[1])
    return lax.all_to_all(split, ("y", "z"), 0, 0, tiled=True).reshape(packed.shape)


def body(hidden_states, expert_ids, probs, cotangent, w_gate, w_up, w_down):
    parts = lax.axis_size("mp")
    tokens = hidden_states.shape[0]
    hidden_rows, model_width = w_gate.shape
    ids_row, probs_row = expert_ids.reshape(1, tokens), probs.reshape(1, tokens)
    x_own, s_own = unpack(over_yz(send(ids_row, probs_row, hidden_states, cotangent)))
    x_other, s_other = swap_cores(x_own), swap_cores(s_own)
    x_behind, x_behind_other = ring(x_own), ring(x_other)
    s_behind, s_behind_other = ring(s_own), ring(s_other)
    x_opposite, s_opposite = ring(x_behind), ring(s_behind)
    x_first, s_first = (x_own, x_other, x_behind, x_behind_other), (s_own, s_other, s_behind, s_behind_other)
    slots, width = x_own.shape
    pair = 2 * slots
    act = jax.ShapeDtypeStruct((pair, hidden_rows), F32)
    act16 = jax.ShapeDtypeStruct((pair, hidden_rows), BF16)
    sums = (jax.ShapeDtypeStruct((slots, width), BF16),) * (2 * parts)
    weight = jax.ShapeDtypeStruct(w_gate.shape, BF16)
    product = 2 * pair * hidden_rows * model_width
    moved = 2 * hidden_rows * model_width
    weights = (w_gate, w_up, w_down)
    waited = after(x_behind_other, s_behind)
    gate, up = kernel_call(functools.partial(first_x_kernel, parts), (act, act), product, 3 * moved)(
        *x_first[:3], waited, *weights
    )
    grad = kernel_call(functools.partial(first_s_kernel, parts), act, product // 2, moved)(*s_first, w_down)
    x_rest = (swap_cores(x_behind_other), swap_cores(x_behind), x_opposite, swap_cores(after(x_opposite, gate, grad)))
    s_rest = (swap_cores(s_behind_other), swap_cores(s_behind), s_opposite, swap_cores(after(s_opposite, grad)))
    gate, up, gated, *out = kernel_call(
        functools.partial(forward_kernel, parts), (act, act, act16) + sums, 2 * product, 5 * moved
    )(*x_rest, *weights, gate, up)
    out_tail, out_other = ring_inputs(*out)
    wider = (jax.ShapeDtypeStruct((slots, width + LANES), BF16),) * (2 * parts)
    ggp, gup, *dx = kernel_call(
        functools.partial(backward_kernel, parts), (act16, act16) + wider, 5 * product // 2, 5 * moved
    )(*s_rest, *weights, gate, up, gated, grad)
    out_sum, _ = summed(out, out_tail, out_other)
    dx_sum, last = summed(dx, *ring_inputs(*dx))
    grads = kernel_call(functools.partial(weights_kernel, parts), (weight, weight, weight), 3 * product, 6 * moved)(
        *x_first, *x_rest, *s_first, *s_rest, after(ggp, last), gup, gated
    )
    dx_sum = (dx_sum[0], after(dx_sum[1], grads[0]), dx_sum[2])
    packed = jax.ShapeDtypeStruct((EXPERTS * ROOM * TILE, LANES), BF16)
    packed = kernel_call(return_kernel, packed, 4 * packed.size * LANES, 8 * packed.size)(*out_sum, *dx_sum)
    mixed, grad_hidden, grad_row = home(ids_row, probs_row, over_yz(packed))
    grad_probs = grad_row.reshape(tokens, 1)
    return (mixed, grad_hidden, grad_probs, *grads)


def solution(mesh):
    yz_core = mesh.devices.shape[0]
    cores = 2
    columns_count = EXPERTS
    rows_y = 4
    grid = Mesh(
        mesh.devices.reshape(rows_y, yz_core // (cores * rows_y), cores, mesh.devices.shape[1]),
        ("y", "z", "core", "mp"),
    )
    assert yz_core == columns_count * cores
    blk = ("y", "z", "core")
    wide, thin, weight = P(blk, "mp"), P(blk, None), P(blk + ("mp",), None)
    return jax.shard_map(
        body,
        mesh=grid,
        in_specs=(wide, thin, thin, wide, weight, weight, weight),
        out_specs=(wide, wide, thin, weight, weight, weight),
        check_vma=False,
    )
```

```python
import functools

import jax
import jax.numpy as jnp
from jax import lax
from jax.experimental import pallas as pl
from jax.experimental.pallas import tpu as pltpu
from jax.sharding import Mesh, PartitionSpec as P

EXPERTS = 32
CAP = 5
ROOM = CAP + 1
LANES = 128
TILE = 16
F32 = jnp.float32
BF16 = jnp.bfloat16
VMEM_LIMIT = 12 * 1024 * 1024
SEND_LIMIT = 56 * 1024 * 1024


def dot(a, b, contract=((1,), (0,))):
    return lax.dot_general(a, b, (contract, ((), ())), preferred_element_type=F32)


def kernel_call(body, out_shape, flops, moved):
    def call(*args):
        specs = [pl.BlockSpec(memory_space=pltpu.VMEM)] * len(args)
        return pl.pallas_call(
            body,
            name=getattr(body, "func", body).__name__,
            out_shape=out_shape,
            in_specs=specs,
            out_specs=jax.tree.map(lambda _: pl.BlockSpec(memory_space=pltpu.VMEM), out_shape),
            compiler_params=pltpu.CompilerParams(vmem_limit_bytes=VMEM_LIMIT),
            cost_estimate=pl.CostEstimate(flops=flops, bytes_accessed=moved, transcendentals=0),
        )(*args)

    return call


def exchange_matrix():
    n = TILE * TILE
    out_row = lax.broadcasted_iota(jnp.int32, (n, n), 0)
    in_row = lax.broadcasted_iota(jnp.int32, (n, n), 1)
    return (in_row == (out_row % TILE) * TILE + out_row // TILE).astype(BF16)


def pack_rows(left, right, packed_ref, swap=None):
    swap = exchange_matrix() if swap is None else swap
    rows = TILE * TILE
    for group in range(packed_ref.shape[0] // rows):
        parts = [side[group * TILE : (group + 1) * TILE] for side in (left, right)]
        stacked = [part[:, j * LANES : (j + 1) * LANES] for part in parts for j in range(TILE // 2)]
        packed_ref[pl.ds(group * rows, rows), :] = dot(swap, jnp.concatenate(stacked, axis=0)).astype(BF16)


def unpack_rows(packed_ref, wide_refs):
    swap = exchange_matrix()
    rows = TILE * TILE
    for group in range(packed_ref.shape[0] // rows):
        value = dot(swap, packed_ref[pl.ds(group * rows, rows), :]).astype(BF16)
        for at, wide in wide_refs.items():
            for j in range(TILE // 2):
                q = (at * (TILE // 2) + j) * TILE
                wide[pl.ds(group * TILE, TILE), pl.ds(j * LANES, LANES)] = value[q : q + TILE]


def token_ranks(ids_row):
    tokens = ids_row.shape[1]
    expert = lax.broadcasted_iota(jnp.int32, (EXPERTS, tokens), 0)
    onehot = (expert == ids_row).astype(F32)
    before = lax.broadcasted_iota(jnp.int32, (tokens, tokens), 0)
    token = lax.broadcasted_iota(jnp.int32, (tokens, tokens), 1)
    earlier = (before < token).astype(BF16)
    counts = dot(onehot.astype(BF16), earlier)
    return jnp.sum(counts * onehot, axis=0, keepdims=True).astype(jnp.int32)


def placement(ids_row, ranks, room):
    slot = lax.broadcasted_iota(jnp.int32, (EXPERTS * room, ids_row.shape[1]), 0)
    return (slot == ids_row * room + ranks).astype(BF16)


def column(row):
    return jnp.transpose(jnp.broadcast_to(row.astype(F32), (LANES, row.shape[1])))[:, :1]


def column(row):
    return jnp.transpose(jnp.broadcast_to(row.astype(F32), (LANES, row.shape[1])))[:, :1]


def send_kernel(ids_hbm, probs_hbm, hidden_hbm, cotangent_hbm, packed_ref, ids, probs, hidden, cotangent, sems):
    pairs = ((ids_hbm, ids), (probs_hbm, probs), (hidden_hbm, hidden), (cotangent_hbm, cotangent))
    copies = [pltpu.make_async_copy(*pair, sems.at[at]) for at, pair in enumerate(pairs)]
    for copy in copies:
        copy.start()
    swap = exchange_matrix()
    copies[0].wait()
    select = placement(ids[...], token_ranks(ids[...]), CAP)
    copies[2].wait()
    left = dot(select, hidden[...]).astype(BF16)
    copies[1].wait()
    copies[3].wait()
    scaled = (column(probs[...]) * cotangent[...].astype(F32)).astype(BF16)
    pack_rows(left, dot(select, scaled).astype(BF16), packed_ref, swap)


def send(*args):
    return pl.pallas_call(
        send_kernel,
        name="send",
        out_shape=jax.ShapeDtypeStruct((EXPERTS * CAP * TILE, LANES), BF16),
        in_specs=[pl.BlockSpec(memory_space=pltpu.HBM)] * len(args),
        out_specs=pl.BlockSpec(memory_space=pltpu.VMEM),
        scratch_shapes=[pltpu.VMEM(a.shape, a.dtype) for a in args] + [pltpu.SemaphoreType.DMA((len(args),))],
        compiler_params=pltpu.CompilerParams(vmem_limit_bytes=SEND_LIMIT),
    )(*args)


def unpack_kernel(packed_ref, x_ref, s_ref):
    unpack_rows(packed_ref, {0: x_ref, 1: s_ref})


def unpack(packed):
    out = jax.ShapeDtypeStruct((packed.shape[0] // TILE, TILE * LANES // 2), BF16)
    return kernel_call(unpack_kernel, (out, out), 4 * packed.size * LANES, 8 * packed.size)(packed)


def blocks(parts):
    mp, core = lax.axis_index("mp"), lax.axis_index("core")
    ahead = 1 + (parts - 2) * core
    return [lax.rem(mp + step, parts) for step in (0, parts - ahead, ahead, parts // 2)]


def columns(ref, block, parts):
    width = ref.shape[1] // parts
    return pl.ds(pl.multiple_of(block * width, width), width)


def held(own, other):
    return jnp.concatenate([own[...], other[...]], axis=0)


def write_shards(values, refs):
    for at, value in enumerate(values):
        half = value.shape[0] // 2
        refs[2 * at][...] = value[:half]
        refs[2 * at + 1][...] = value[half:]


def first_x_kernel(parts, own, own_other, behind, behind_other, wg, wu, wd, gate_ref, up_ref):
    gate, up = 0.0, 0.0
    for block, mine, other in zip(blocks(parts), (own, behind), (own_other, behind_other)):
        at = columns(wg, block, parts)
        x = held(mine, other)
        gate = gate + dot(x, wg[:, at], ((1,), (1,)))
        up = up + dot(x, wu[:, at], ((1,), (1,)))
    gate_ref[...] = gate
    up_ref[...] = up


def first_s_kernel(parts, own, own_other, behind, behind_other, wd, grad_ref):
    grad = 0.0
    for block, mine, other in zip(blocks(parts), (own, behind), (own_other, behind_other)):
        grad = grad + dot(held(mine, other), wd[:, columns(wd, block, parts)], ((1,), (1,)))
    grad_ref[...] = grad


def forward_kernel(parts, *refs):
    shards, (wg, wu, wd, gate_in, up_in, gate_ref, up_ref, gated_ref), out = refs[:4], refs[4:12], refs[12:]
    places = blocks(parts)
    gate, up = gate_in[...], up_in[...]
    for at in range(2):
        cut = columns(wg, places[2 + at], parts)
        x = held(shards[2 * at], shards[2 * at + 1])
        gate = gate + dot(x, wg[:, cut], ((1,), (1,)))
        up = up + dot(x, wu[:, cut], ((1,), (1,)))
    gate_ref[...] = gate
    up_ref[...] = up
    gated = (gate * (1.0 / (1.0 + jnp.exp(-gate))) * up).astype(BF16)
    gated_ref[...] = gated
    write_shards([dot(gated, wd[:, columns(wd, block, parts)]).astype(BF16) for block in places], out)


def backward_kernel(parts, *refs):
    shards, (wg, wu, wd, gate_ref, up_ref, gated_ref, grad_in, ggp_ref, gup_ref), dx = refs[:4], refs[4:13], refs[13:]
    places = blocks(parts)
    grad = grad_in[...]
    for at in range(2):
        cut = columns(wd, places[2 + at], parts)
        grad = grad + dot(held(shards[2 * at], shards[2 * at + 1]), wd[:, cut], ((1,), (1,)))
    terms = jnp.sum(grad * gated_ref[...].astype(F32), axis=1, keepdims=True)
    terms = jnp.broadcast_to(terms, (terms.shape[0], LANES)).astype(BF16)
    gate = gate_ref[...]
    sigmoid = 1.0 / (1.0 + jnp.exp(-gate))
    ggp = (grad * up_ref[...] * sigmoid * (1.0 + gate * (1.0 - sigmoid))).astype(BF16)
    gup = (grad * (gate * sigmoid)).astype(BF16)
    ggp_ref[...] = ggp
    gup_ref[...] = gup
    values = []
    for block in places:
        at = columns(wg, block, parts)
        value = (dot(ggp, wg[:, at]) + dot(gup, wu[:, at])).astype(BF16)
        values.append(jnp.concatenate([value, terms], axis=1))
    write_shards(values, dx)


def weights_kernel(parts, *refs):
    x_shards, s_shards, (ggp_ref, gup_ref, gated_ref, gwg, gwu, gwd) = refs[:8], refs[8:16], refs[16:]
    rows = ((0,), (0,))
    for step, block in enumerate(blocks(parts)):
        at = columns(gwg, block, parts)
        x, s = (held(side[2 * step], side[2 * step + 1]) for side in (x_shards, s_shards))
        gwg[:, at] = dot(ggp_ref[...], x, rows).astype(BF16)
        gwu[:, at] = dot(gup_ref[...], x, rows).astype(BF16)
        gwd[:, at] = dot(gated_ref[...], s, rows).astype(BF16)


def add(*terms):
    value = terms[0].astype(F32)
    for term in terms[1:]:
        value = value + term.astype(F32)
    return value.astype(BF16)


def slot_parts(shape, axis, room):
    slot = lax.broadcasted_iota(jnp.int32, shape, axis)
    expert = jnp.floor((slot.astype(F32) + 0.5) * (1.0 / room)).astype(jnp.int32)
    return expert, slot - expert * room


def return_kernel(*refs):
    out, dx, packed_ref = refs[:3], refs[3:6], refs[6]
    width = out[0].shape[1]
    slots, wide = EXPERTS * CAP, EXPERTS * ROOM
    row_expert, row_place = slot_parts((wide, slots), 0, ROOM)
    expert, place = slot_parts((wide, slots), 1, CAP)
    same = row_expert == expert
    spread = (same & (row_place == place)).astype(BF16)
    last = (same & (row_place == CAP)).astype(BF16)
    _, lane_place = slot_parts((slots, LANES), 0, CAP)
    lane = lax.broadcasted_iota(jnp.int32, (slots, LANES), 1)
    sums = add(*(term[...] for term in dx))
    terms = jnp.where(lane_place == lane, sums[:, width:].astype(F32), 0.0).astype(BF16)
    left = dot(spread, add(*(term[...] for term in out)))
    left = jnp.concatenate([left[:, :LANES] + dot(last, terms), left[:, LANES:]], axis=1)
    pack_rows(left.astype(BF16), dot(spread, sums[:, :width]).astype(BF16), packed_ref)


def home_kernel(ids_ref, probs_ref, packed_ref, mixed_ref, hidden_ref, grad_ref, out_wide, dx_wide):
    ids = ids_ref[...]
    ranks = token_ranks(ids)
    select = placement(ids, ranks, ROOM)
    unpack_rows(packed_ref, {0: out_wide, 1: dx_wide})
    rows = ((0,), (0,))
    probs = column(probs_ref[...])
    mixed_ref[...] = (probs * dot(select, out_wide[...], rows)).astype(BF16)
    hidden_ref[...] = dot(select, dx_wide[...], rows).astype(BF16)
    last = placement(ids, jnp.full_like(ranks, CAP), ROOM)
    parts = dot(last, out_wide[:, :LANES], rows)
    lane = lax.broadcasted_iota(jnp.int32, (ids.shape[1], LANES), 1)
    terms = jnp.where(lane == column(ranks).astype(jnp.int32), parts, 0.0)
    grad = jnp.sum(terms, axis=1, keepdims=True) / probs
    grad_ref[...] = jnp.transpose(jnp.broadcast_to(grad, (grad.shape[0], LANES)))[:1]


def home(ids_row, probs_row, packed):
    slots, width, tokens = packed.shape[0] // TILE, TILE * LANES // 2, ids_row.shape[1]
    wide = jax.ShapeDtypeStruct((tokens, width), BF16)
    return pl.pallas_call(
        home_kernel,
        name="home",
        out_shape=(wide, wide, jax.ShapeDtypeStruct((1, tokens), F32)),
        in_specs=[pl.BlockSpec(memory_space=pltpu.VMEM)] * 3,
        scratch_shapes=[pltpu.VMEM((slots, width), BF16)] * 2,
        compiler_params=pltpu.CompilerParams(vmem_limit_bytes=VMEM_LIMIT),
    )(ids_row, probs_row, packed)


def shift(value, axis, step):
    count = lax.axis_size(axis)
    return lax.ppermute(value, axis, [(i, (i + step) % count) for i in range(count)])


def swap_cores(value):
    return shift(value, "core", 1)


def ring(value):
    count = lax.axis_size("mp")
    pairs = [(i, (i + 1) % count) for i in range(count)]
    pairs += [(count + i, count + (i - 1) % count) for i in range(count)]
    return lax.ppermute(value, ("core", "mp"), pairs)


def after(value, *first):
    return lax.optimization_barrier((value, *first))[0]


def ring_inputs(own, own_other, behind, behind_other, ahead, ahead_other, opposite, opposite_other):
    return add(opposite, swap_cores(opposite_other)), add(ahead_other, swap_cores(behind))


def summed(terms, tail, other):
    own, own_other, _, behind_other, ahead, *_ = terms
    came_other = ring(other)
    last = add(ahead, swap_cores(behind_other), ring(tail))
    return (own, ring(last), swap_cores(add(own_other, came_other))), last


def over_yz(packed):
    parts = lax.axis_size("y") * lax.axis_size("z")
    split = packed.reshape(parts, packed.shape[0] // parts, packed.shape[1])
    return lax.all_to_all(split, ("y", "z"), 0, 0, tiled=True).reshape(packed.shape)


def body(hidden_states, expert_ids, probs, cotangent, w_gate, w_up, w_down):
    parts = lax.axis_size("mp")
    tokens = hidden_states.shape[0]
    hidden_rows, model_width = w_gate.shape
    ids_row, probs_row = expert_ids.reshape(1, tokens), probs.reshape(1, tokens)
    x_own, s_own = unpack(over_yz(send(ids_row, probs_row, hidden_states, cotangent)))
    x_other, s_other = swap_cores(x_own), swap_cores(s_own)
    x_behind, x_behind_other = ring(x_own), ring(x_other)
    s_behind, s_behind_other = ring(s_own), ring(s_other)
    x_opposite, s_opposite = ring(x_behind), ring(s_behind)
    x_first, s_first = (x_own, x_other, x_behind, x_behind_other), (s_own, s_other, s_behind, s_behind_other)
    slots, width = x_own.shape
    pair = 2 * slots
    act = jax.ShapeDtypeStruct((pair, hidden_rows), F32)
    act16 = jax.ShapeDtypeStruct((pair, hidden_rows), BF16)
    sums = (jax.ShapeDtypeStruct((slots, width), BF16),) * (2 * parts)
    weight = jax.ShapeDtypeStruct(w_gate.shape, BF16)
    product = 2 * pair * hidden_rows * model_width
    moved = 2 * hidden_rows * model_width
    weights = (w_gate, w_up, w_down)
    waited = after(x_behind_other, s_behind)
    gate, up = kernel_call(functools.partial(first_x_kernel, parts), (act, act), product, 3 * moved)(
        *x_first[:3], waited, *weights
    )
    grad = kernel_call(functools.partial(first_s_kernel, parts), act, product // 2, moved)(*s_first, w_down)
    x_rest = (swap_cores(x_behind_other), swap_cores(x_behind), x_opposite, swap_cores(after(x_opposite, gate)))
    s_rest = (swap_cores(s_behind_other), swap_cores(s_behind), s_opposite, swap_cores(after(s_opposite, grad)))
    gate, up, gated, *out = kernel_call(
        functools.partial(forward_kernel, parts), (act, act, act16) + sums, 2 * product, 5 * moved
    )(*x_rest, *weights, gate, up)
    out_tail, out_other = ring_inputs(*out)
    wider = (jax.ShapeDtypeStruct((slots, width + LANES), BF16),) * (2 * parts)
    ggp, gup, *dx = kernel_call(
        functools.partial(backward_kernel, parts), (act16, act16) + wider, 5 * product // 2, 5 * moved
    )(*s_rest, *weights, gate, up, gated, grad)
    out_sum, _ = summed(out, out_tail, out_other)
    dx_sum, last = summed(dx, *ring_inputs(*dx))
    grads = kernel_call(functools.partial(weights_kernel, parts), (weight, weight, weight), 3 * product, 6 * moved)(
        *x_first, *x_rest, *s_first, *s_rest, after(ggp, last), gup, gated
    )
    dx_sum = (dx_sum[0], after(dx_sum[1], grads[0]), dx_sum[2])
    packed = jax.ShapeDtypeStruct((EXPERTS * ROOM * TILE, LANES), BF16)
    packed = kernel_call(return_kernel, packed, 4 * packed.size * LANES, 8 * packed.size)(*out_sum, *dx_sum)
    mixed, grad_hidden, grad_row = home(ids_row, probs_row, over_yz(packed))
    grad_probs = grad_row.reshape(tokens, 1)
    return (mixed, grad_hidden, grad_probs, *grads)


def solution(mesh):
    yz_core = mesh.devices.shape[0]
    cores = 2
    columns_count = EXPERTS
    rows_y = 4
    grid = Mesh(
        mesh.devices.reshape(rows_y, yz_core // (cores * rows_y), cores, mesh.devices.shape[1]),
        ("y", "z", "core", "mp"),
    )
    assert yz_core == columns_count * cores
    blk = ("y", "z", "core")
    wide, thin, weight = P(blk, "mp"), P(blk, None), P(blk + ("mp",), None)
    return jax.shard_map(
        body,
        mesh=grid,
        in_specs=(wide, thin, thin, wide, weight, weight, weight),
        out_specs=(wide, wide, thin, weight, weight, weight),
        check_vma=False,
    )
```
